128 devices in a mesh: dp: 16 (over y, z_hi, core), fsdp: 8 (over z_lo, x).
Axes of the slice: x: 4, y: 4, z: 4 (z_hi: 2, z_lo: 2; z = z_hi * 2 + z_lo), core: 2. Of those that a mesh axis runs over, the one named last changes fastest.
Arguments:
- tokens: bfloat16 [65536, 8192], P(('dp', 'fsdp')), may hold values from -24 to 24
- cotangent: bfloat16 [65536, 1024], P(('dp', 'fsdp')), may hold values from -0.0625 to 0.0625
- weight: bfloat16 [8192, 1024], P('fsdp'), may hold values from -0.0625 to 0.0625
- basis: bfloat16 [1024, 512], replicated, may hold values from -0.1875 to 0.1875
- exp_avg: float32 [8192, 512], P(('fsdp', 'dp')), may hold values from -4 to 4
- exp_avg_sq: float32 [8192, 512], P(('fsdp', 'dp')), may hold values from 0.01 to 1
Outputs:
- keys: bfloat16 [65536, 1024], P(('dp', 'fsdp'))
- new_weight: bfloat16 [8192, 1024], P('fsdp')
- new_avg: float32 [8192, 512], P(('fsdp', 'dp'))
- new_sq: float32 [8192, 512], P(('fsdp', 'dp'))
The draws below stay inside these ranges and needn't reach their ends.
All inputs are finite; a program needn't handle non-finite values.
Results may differ from the reference program's by a relative error of at most 0.0065.
Values may be sent and summed in bfloat16 or wider, within the bound.
No kernel may reach another device: no remote copies, remote signals or barrier semaphores. Data moves between devices by JAX's collectives and lax.ppermute only.
A program may use at most 128 MiB of HBM per device.

```python
import math
import jax
import jax.numpy as jnp
from jax import lax

D = 8192
RANK = 512
STEP = 100
KV = 1024
TOKENS = 65536


def strengthened(drawn, key, source, target, blocks, factor):
    owner, partner = [(jnp.arange(drawn.shape[position]) // (drawn.shape[position] // blocks)).reshape([-1 if axis == position else 1 for axis in range(drawn.ndim)]) for position in (source, target)]
    chosen = jax.random.permutation(key, blocks)[partner]
    strong = (owner == chosen) | (owner == (partner + blocks // 2) % blocks)
    return jnp.where(strong, factor * drawn, drawn)


def level_of(rng, extent, shards, least, largest):
    loudness, own = 1.0, jax.random.fold_in(rng, 6)
    for dim, parts in shards:
        draws = jnp.exp(jax.random.uniform(jax.random.fold_in(own, dim), (parts,), jnp.float32, least / len(shards), largest / len(shards)))
        loudness = loudness * jnp.repeat(draws, extent[dim] // parts).reshape([-1 if axis == dim else 1 for axis in range(len(extent))])
    return loudness


def centred(own_key, shape, scale, bound, pieces=(), kind=jnp.bfloat16):
    loudness = level_of(own_key, shape, pieces, -0.22, 0.18) if pieces else 1.0
    result = jax.random.normal(own_key, shape, jnp.float32) * scale * loudness
    return jnp.minimum(jnp.maximum(result, -bound), bound).astype(kind)


def gaussian_with(rng, extent, spread, reach, shards, heavy, kind=jnp.bfloat16):
    drawn = spread * jax.random.normal(rng, extent, jnp.float32)
    if shards:
        drawn = drawn * level_of(rng, extent, shards, -0.22, 0.18)
    return jnp.clip(strengthened(drawn, jax.random.fold_in(rng, 3), *heavy), -reach, reach).astype(kind)


def setup_inputs(seed: int = 0) -> dict:
    streams_of = jax.random.split(jax.random.key(seed), 7)
    return {
        "tokens": gaussian_with(streams_of[0], (TOKENS, D), 1.0, 24.0, ((0, 128),), (0, 1, 128, 5.5)),
        "cotangent": centred(streams_of[1], (TOKENS, KV), (TOKENS ** -0.5), 0.0625, ((0, 128),)),
        "weight": centred(streams_of[2], (D, KV), D ** -0.5, 0.0625, ((0, 8),)),
        "basis": centred(streams_of[3], (KV, RANK), KV ** -0.5, 0.1875),
        "exp_avg": centred(streams_of[4], (D, RANK), 0.3, 4.0, ((0, 128),), jnp.float32),
        "exp_avg_sq": jnp.clip(jnp.exp(math.log(1.0) - 4.6051702 * jax.random.uniform(streams_of[5], (D, RANK), jnp.float32) ** level_of(streams_of[5], (D, RANK), ((0, 128),), -0.2, 0.2)), 0.01, 1.0),
    }


learn_rate = 0.01
galore_scale = 0.25

def reference(tokens, cotangent, weight, basis, exp_avg, exp_avg_sq):
    keys = jnp.dot(tokens, weight, preferred_element_type=jnp.float32).astype(jnp.bfloat16)
    low = jnp.dot(cotangent, basis, preferred_element_type=jnp.float32).astype(jnp.bfloat16)
    projected = jnp.dot(tokens.T, low, preferred_element_type=jnp.float32)
    new_avg = 0.9 * exp_avg + 0.1 * projected
    new_sq = 0.999 * exp_avg_sq + 0.001 * projected * projected
    first_fix = 1.0 - 0.9 ** STEP
    second_fix = 1.0 - 0.999 ** STEP
    direction = new_avg / first_fix / (jnp.sqrt(new_sq / second_fix) + 1e-08)
    update = lax.dot_general(direction, basis.astype(jnp.float32), (((1,), (1,)), ((), ())), precision=lax.Precision.HIGHEST)
    new_weight = (weight.astype(jnp.float32) - learn_rate * galore_scale * update).astype(jnp.bfloat16)
    return (keys, new_weight, new_avg, new_sq)
```

```python
import jax
import jax.numpy as jnp
from jax import lax
from jax.experimental import pallas as pl
from jax.experimental.pallas import tpu as pltpu
from jax.sharding import PartitionSpec as P

STEP = 100
AXES = ("dp", "fsdp")

learn_rate = 0.01
galore_scale = 0.25

ROWS = 64
VMEM = 48 * 1024 * 1024


def pack_columns(parity, tokens):
    count, width = tokens.shape
    blocks = 8
    wide = width // blocks

    def body(parity_ref, x_ref, o_ref):
        row = lax.broadcasted_iota(jnp.int32, (256, 128), 0)
        col = lax.broadcasted_iota(jnp.int32, (256, 128), 1)
        chosen = col + jnp.where(col >= 64, 64, 0) + parity_ref[0] * 64
        select = jnp.where(row == chosen, 1.0, 0.0).astype(jnp.bfloat16)
        for j in range(wide // 256):
            o_ref[0, :, j * 128 : (j + 1) * 128] = jnp.dot(
                x_ref[:, j * 256 : (j + 1) * 256], select, preferred_element_type=jnp.float32
            ).astype(jnp.bfloat16)

    return pl.pallas_call(
        body,
        grid_spec=pltpu.PrefetchScalarGridSpec(
            num_scalar_prefetch=1,
            grid=(blocks,),
            in_specs=[pl.BlockSpec((count, wide), lambda f, p: (0, f))],
            out_specs=pl.BlockSpec((1, count, wide // 2), lambda f, p: (f, 0, 0)),
        ),
        out_shape=jax.ShapeDtypeStruct((blocks, count, wide // 2), jnp.bfloat16),
        compiler_params=pltpu.CompilerParams(vmem_limit_bytes=VMEM),
        cost_estimate=pl.CostEstimate(flops=2 * count * width * 128, bytes_accessed=3 * count * width, transcendentals=0),
        name="pack_columns",
    )(parity, tokens)


def partial_gradient(own, other, low, low_other):
    blocks, count, wide = own.shape
    rank = low.shape[1]
    parts = wide // ROWS
    contract = (((0,), (0,)), ((), ()))

    def body(a_ref, b_ref, la_ref, lb_ref, o_ref):
        total = lax.dot_general(a_ref[0], la_ref[...], contract, preferred_element_type=jnp.float32)
        total = total + lax.dot_general(b_ref[0], lb_ref[...], contract, preferred_element_type=jnp.float32)
        o_ref[...] = total.reshape(parts, 1, ROWS, rank).astype(jnp.bfloat16)

    piece = pl.BlockSpec((1, count, wide), lambda f: (f, 0, 0))
    whole = pl.BlockSpec((count, rank), lambda f: (0, 0))
    return pl.pallas_call(
        body,
        grid=(blocks,),
        in_specs=[piece, piece, whole, whole],
        out_specs=pl.BlockSpec((parts, 1, ROWS, rank), lambda f: (0, f, 0, 0)),
        out_shape=jax.ShapeDtypeStruct((parts, blocks, ROWS, rank), jnp.bfloat16),
        compiler_params=pltpu.CompilerParams(vmem_limit_bytes=VMEM),
        cost_estimate=pl.CostEstimate(
            flops=4 * blocks * count * wide * rank, bytes_accessed=6 * blocks * count * wide, transcendentals=0
        ),
        name="partial_gradient",
    )(own, other, low, low_other)


def keys_partial(packed, weight, addend=None):
    blocks, count, wide = packed.shape
    features = weight.shape[1]

    def body(x_ref, w_ref, *refs):
        f = pl.program_id(0)
        acc_ref = refs[-1]
        product = jnp.dot(x_ref[0], w_ref[...], preferred_element_type=jnp.float32)

        @pl.when(f == 0)
        def _():
            acc_ref[...] = product if addend is None else product + refs[0][...]

        @pl.when(f > 0)
        def _():
            acc_ref[...] += product

        if addend is not None:

            @pl.when(f == blocks - 1)
            def _():
                refs[1][...] = acc_ref[...].astype(jnp.bfloat16)

    whole = pl.BlockSpec((count, features), lambda f: (0, 0))
    specs = [
        pl.BlockSpec((1, count, wide), lambda f: (f, 0, 0)),
        pl.BlockSpec((wide, features), lambda f: (f, 0)),
    ]
    kind = jnp.float32 if addend is None else jnp.bfloat16
    return pl.pallas_call(
        body,
        grid=(blocks,),
        in_specs=specs + ([] if addend is None else [whole]),
        out_specs=whole,
        out_shape=jax.ShapeDtypeStruct((count, features), kind),
        scratch_shapes=[] if addend is None else [pltpu.VMEM((count, features), jnp.float32)],
        compiler_params=pltpu.CompilerParams(vmem_limit_bytes=VMEM),
        cost_estimate=pl.CostEstimate(
            flops=2 * blocks * count * wide * features,
            bytes_accessed=2 * blocks * wide * (count + features),
            transcendentals=0,
        ),
        name="keys_partial",
    )(*([packed, weight] + ([] if addend is None else [addend])))


def local(tokens, cotangent, weight, basis, exp_avg, exp_avg_sq):
    fsdp_size = lax.axis_size("fsdp")
    dp_size = lax.axis_size("dp")
    core = lax.axis_index("dp") % 2
    chips = dp_size // 2
    features = weight.shape[1]
    swap = [
        (d * fsdp_size + f, (d + 1 - 2 * (d % 2)) * fsdp_size + f) for d in range(dp_size) for f in range(fsdp_size)
    ]
    same_core = [
        [(2 * q + c) * fsdp_size + f for q in range(chips) for f in range(fsdp_size)] for c in range(2)
    ]
    shard_chips = [[(2 * q + c) * fsdp_size + f for q in range(chips)] for c in range(2) for f in range(fsdp_size)]

    send = pack_columns((1 - core).reshape(1), tokens)
    other = lax.ppermute(send, AXES, swap)
    low = jnp.dot(cotangent, basis, preferred_element_type=jnp.float32).astype(jnp.bfloat16)
    low_other = lax.ppermute(low, AXES, swap)
    own = pack_columns(core.reshape(1), tokens)

    rows = weight.reshape(chips, 2, ROWS, features)
    half = lax.dynamic_index_in_dim(rows, core, 1, keepdims=False)
    gathered = lax.all_gather(half.reshape(chips * ROWS, features), "fsdp", axis=0, tiled=True)

    partial = partial_gradient(own, other, low, low_other)
    spread = lax.all_to_all(
        partial.reshape(chips * fsdp_size, ROWS, partial.shape[-1]),
        AXES,
        split_axis=0,
        concat_axis=0,
        axis_index_groups=same_core,
        tiled=True,
    )
    projected = jnp.sum(spread.astype(jnp.float32), axis=0)
    new_avg = 0.9 * exp_avg + 0.1 * projected
    new_sq = 0.999 * exp_avg_sq + 0.001 * projected * projected
    first_fix = 1.0 - 0.9**STEP
    second_fix = 1.0 - 0.999**STEP
    direction = new_avg / first_fix / (jnp.sqrt(new_sq / second_fix) + 1e-08)
    update = lax.dot_general(
        direction,
        basis.astype(jnp.float32),
        (((1,), (1,)), ((), ())),
        precision=lax.Precision.HIGHEST,
    )
    place = lax.axis_index("dp") * ROWS
    own_rows = lax.dynamic_slice_in_dim(weight, place, ROWS, 0)
    fresh = (own_rows.astype(jnp.float32) - learn_rate * galore_scale * update).astype(jnp.bfloat16)
    mine = lax.all_to_all(
        jnp.broadcast_to(fresh[None], (chips, ROWS, features)),
        AXES,
        split_axis=0,
        concat_axis=0,
        axis_index_groups=shard_chips,
        tiled=True,
    )
    theirs = lax.ppermute(mine, AXES, swap)
    first = jnp.where(core == 0, mine, theirs)
    second = jnp.where(core == 0, theirs, mine)
    new_weight = jnp.stack([first, second], axis=1).reshape(weight.shape)

    for_other = keys_partial(other, gathered)
    from_other = lax.ppermute(for_other, AXES, swap)
    keys = keys_partial(own, gathered, from_other)
    return (keys, new_weight, new_avg, new_sq)


def solution(mesh):
    in_specs = (
        P(("dp", "fsdp"), None),
        P(("dp", "fsdp"), None),
        P("fsdp", None),
        P(),
        P(("fsdp", "dp"), None),
        P(("fsdp", "dp"), None),
    )
    out_specs = (
        P(("dp", "fsdp"), None),
        P("fsdp", None),
        P(("fsdp", "dp"), None),
        P(("fsdp", "dp"), None),
    )
    return jax.shard_map(local, mesh=mesh, in_specs=in_specs, out_specs=out_specs, check_vma=False)
```

```python
import jax
import jax.numpy as jnp
from jax import lax
from jax.experimental import pallas as pl
from jax.experimental.pallas import tpu as pltpu
from jax.sharding import PartitionSpec as P

STEP = 100
AXES = ("dp", "fsdp")

learn_rate = 0.01
galore_scale = 0.25

ROWS = 64
VMEM = 48 * 1024 * 1024


CORE, LO, X = 2, 2, 4
PAIR = 2 * ROWS


def pack_columns(place, tokens):
    count, width = tokens.shape
    steps = 4
    tall = count // steps

    def body(place_ref, x_ref, own_ref, send_ref):
        for now in range(2):

            @pl.when(place_ref[0] == now)
            def _():
                for j, (y, shard) in enumerate((y, shard) for y in range(4) for shard in range(LO * X)):
                    for out_ref, side in ((own_ref, now), (send_ref, 1 - now)):
                        a = shard * (width // (LO * X)) + y * 2 * PAIR + side * ROWS
                        out_ref[:, j * PAIR : (j + 1) * PAIR] = jnp.concatenate(
                            [x_ref[:, a : a + ROWS], x_ref[:, a + PAIR : a + PAIR + ROWS]], axis=1
                        )

    out = jax.ShapeDtypeStruct((count, width // 2), jnp.bfloat16)
    spec = pl.BlockSpec((tall, width // 2), lambda i, c: (i, 0))
    return pl.pallas_call(
        body,
        grid_spec=pltpu.PrefetchScalarGridSpec(
            num_scalar_prefetch=1,
            grid=(steps,),
            in_specs=[pl.BlockSpec((tall, width), lambda i, c: (i, 0))],
            out_specs=[spec, spec],
        ),
        out_shape=[out, out],
        compiler_params=pltpu.CompilerParams(vmem_limit_bytes=VMEM),
        cost_estimate=pl.CostEstimate(flops=1, bytes_accessed=1, transcendentals=0),
        name="pack_columns",
    )(place, tokens)


def pack_rows(place, weight):
    chips, _, rows, features = weight.shape
    steps = 2
    block = chips // steps

    def body(place_ref, w_ref, o_ref):
        o_ref[...] = w_ref[:, place_ref[0]]

    return pl.pallas_call(
        body,
        grid_spec=pltpu.PrefetchScalarGridSpec(
            num_scalar_prefetch=1,
            grid=(steps,),
            in_specs=[pl.BlockSpec((block, 2, rows, features), lambda i, c: (i, 0, 0, 0))],
            out_specs=pl.BlockSpec((block, rows, features), lambda i, c: (i, 0, 0)),
        ),
        out_shape=jax.ShapeDtypeStruct((chips, rows, features), weight.dtype),
        compiler_params=pltpu.CompilerParams(vmem_limit_bytes=VMEM),
        cost_estimate=pl.CostEstimate(flops=1, bytes_accessed=1, transcendentals=0),
        name="pack_rows",
    )(place, weight)


def keys_of(packed, place, near, far):
    _, _, part, features = near.shape
    count = LO * X
    tokens = packed.shape[0]
    depth = count * 4 * part
    wide = features // 4

    def body(place_ref, x_ref, near_ref, far_ref, o_ref, rows_ref, x_now, sems):
        copies = [pltpu.make_async_copy(x_ref, x_now, sems.at[count])]
        for lo, ref in enumerate((near_ref, far_ref)):
            for x in range(X):
                at = lax.rem(place_ref[1] + lo, LO) * X + x
                copies.append(pltpu.make_async_copy(ref.at[x], rows_ref.at[:, at], sems.at[lo * X + x]))
        for copy in copies:
            copy.start()
        for copy in copies:
            copy.wait()
        for n in range(4):
            columns = slice(n * wide, (n + 1) * wide)
            block = rows_ref[:, :, :, columns].reshape(depth, wide)
            o_ref[:, columns] = jnp.dot(x_now[...], block, preferred_element_type=jnp.float32)

    out, joined = pl.pallas_call(
        body,
        grid_spec=pltpu.PrefetchScalarGridSpec(
            num_scalar_prefetch=1,
            grid=(),
            in_specs=[pl.BlockSpec(memory_space=pl.ANY)] * 3,
            out_specs=[pl.BlockSpec(memory_space=pltpu.VMEM)] * 2,
            scratch_shapes=[pltpu.VMEM(packed.shape, packed.dtype), pltpu.SemaphoreType.DMA((count + 1,))],
        ),
        out_shape=[
            jax.ShapeDtypeStruct((tokens, features), jnp.float32),
            jax.ShapeDtypeStruct((4, count, part, features), jnp.bfloat16),
        ],
        compiler_params=pltpu.CompilerParams(vmem_limit_bytes=VMEM),
        cost_estimate=pl.CostEstimate(flops=1, bytes_accessed=1, transcendentals=0),
        name="keys_of",
    )(place, packed, near, far)
    return out, joined.reshape(depth, features)


def together(*arrays, after=()):
    def body(*refs):
        pass

    return pl.pallas_call(
        body,
        in_specs=[pl.BlockSpec(memory_space=pl.ANY)] * (len(arrays) + len(after)),
        out_specs=[pl.BlockSpec(memory_space=pl.ANY)] * len(arrays),
        out_shape=[jax.ShapeDtypeStruct(a.shape, a.dtype) for a in arrays],
        input_output_aliases={i: i for i in range(len(arrays))},
        name="together",
    )(*arrays, *after)


def device(x, y, z, core):
    return ((y % 4) * 4 + (z % 4 >> 1) * 2 + core % 2) * 8 + (z % 2) * 4 + x % 4


def every():
    return [(x, y, z, c) for y in range(4) for z in range(4) for c in range(2) for x in range(4)]


def move(array, x=0, y=0, z=0, core=0):
    return lax.ppermute(
        array, AXES, [(device(*at), device(at[0] + x, at[1] + y, at[2] + z, at[3] + core)) for at in every()]
    )


def move_apart(array, x=0, z=0):
    pairs = []
    for at in every():
        sign = 1 - 2 * at[3]
        pairs.append((device(*at), device(at[0] + sign * x, at[1], at[2] + sign * z, at[3])))
    return lax.ppermute(array, AXES, pairs)


def exchange(array, groups):
    return lax.all_to_all(array, AXES, split_axis=0, concat_axis=0, axis_index_groups=groups, tiled=True)


def local(tokens, cotangent, weight, basis, exp_avg, exp_avg_sq):
    core = lax.axis_index("dp") % 2
    shard = lax.axis_index("fsdp")
    my_lo = shard // X
    my_z = lax.axis_index("dp") // 2 % 2 * 2 + my_lo
    features = weight.shape[1]
    chips = lax.axis_size("dp") // CORE
    rank = basis.shape[1]
    along_y = [[device(x, y, z, c) for y in range(4)] for x in range(4) for z in range(4) for c in range(2)]
    along_x = [[device(x, y, z, c) for x in range(4)] for y in range(4) for z in range(4) for c in range(2)]
    same_shard = [
        [device(x, y, z + 2 * hi, c) for y in range(4) for hi in range(2)]
        for x in range(4)
        for z in range(2)
        for c in range(2)
    ]
    place = jnp.stack([core, my_lo])

    def wide(array):
        return array.astype(jnp.float32)

    own, send = pack_columns(place, tokens)
    other = move(send, core=1)
    low = jnp.dot(cotangent, basis, preferred_element_type=jnp.float32).astype(jnp.bfloat16)
    low_other = move(low, core=1)

    half = pack_rows(place, weight.reshape(chips, CORE, ROWS, features)).reshape(-1, features)
    near = lax.all_gather(half, AXES, axis=0, tiled=True, axis_index_groups=along_x)
    far = move_apart(half, z=-1)

    contract = (((0,), (0,)), ((), ()))
    partial = lax.dot_general(own, low, contract, preferred_element_type=jnp.float32)
    partial = partial + lax.dot_general(other, low_other, contract, preferred_element_type=jnp.float32)
    partial = partial.astype(jnp.bfloat16)

    def sum_all(spread):
        total = wide(spread[0])
        for i in range(1, spread.shape[0]):
            total = total + wide(spread[i])
        return total

    (far,) = together(far, after=(partial,))
    far = lax.all_gather(far, AXES, axis=0, tiled=True, axis_index_groups=along_x)

    def sum_z(parts):
        def take(step):
            z = (my_z + step) % 4
            some = lax.dynamic_slice_in_dim(parts, z % 2, 1, axis=-5)
            some = lax.dynamic_slice_in_dim(some, z // 2, 1, axis=-3)
            return some.reshape(-1, ROWS, parts.shape[-1])

        total = wide(take(0))
        for step in (1, 3, 2):
            total = total + wide(move(take(step), z=step))
        return total.astype(jnp.bfloat16)

    first = partial[:, : rank // 2].reshape(4, -1, rank // 2)
    first = sum_all(exchange(first, along_y)).astype(jnp.bfloat16)
    second = sum_z(partial[:, rank // 2 :].reshape(4, LO, X, 2, ROWS, rank // 2))
    first, second = together(first, second)
    second = sum_all(exchange(second.reshape(4, X * ROWS, rank // 2), along_y)).astype(jnp.bfloat16)
    first = sum_z(first.reshape(LO, X, 2, ROWS, rank // 2))
    both = jnp.concatenate([first.reshape(X, ROWS, -1), second.reshape(X, ROWS, -1)], axis=2)
    projected = sum_all(exchange(both, along_x))
    new_avg = 0.9 * exp_avg + 0.1 * projected
    new_sq = 0.999 * exp_avg_sq + 0.001 * projected * projected
    first_fix = 1.0 - 0.9**STEP
    second_fix = 1.0 - 0.999**STEP
    direction = new_avg / first_fix / (jnp.sqrt(new_sq / second_fix) + 1e-08)
    direction = direction.astype(jnp.bfloat16)
    near, far = (rows.reshape(X, 4, 2 * ROWS, features) for rows in (near, far))
    for_other, rows = keys_of(other, place, near, far)
    own_keys = jnp.dot(own, rows, preferred_element_type=jnp.float32)

    mine = exchange(jnp.broadcast_to(direction[None], (chips, ROWS, rank)), same_shard)
    mine, own_keys = together(mine, own_keys)
    theirs = move(mine, core=1)
    from_other = move(for_other, core=1)
    even = jnp.where(core == 0, mine, theirs)
    odd = jnp.where(core == 0, theirs, mine)
    update = lax.dot_general(
        jnp.stack([even, odd], axis=1).reshape(-1, rank),
        basis,
        (((1,), (1,)), ((), ())),
        preferred_element_type=jnp.float32,
    )
    new_weight = (wide(weight) - learn_rate * galore_scale * update).astype(jnp.bfloat16)
    keys = (own_keys + from_other).astype(jnp.bfloat16)
    return (keys, new_weight, new_avg, new_sq)


def solution(mesh):
    in_specs = (
        P(("dp", "fsdp"), None),
        P(("dp", "fsdp"), None),
        P("fsdp", None),
        P(),
        P(("fsdp", "dp"), None),
        P(("fsdp", "dp"), None),
    )
    out_specs = (
        P(("dp", "fsdp"), None),
        P("fsdp", None),
        P(("fsdp", "dp"), None),
        P(("fsdp", "dp"), None),
    )
    return jax.shard_map(local, mesh=mesh, in_specs=in_specs, out_specs=out_specs, check_vma=False)
```

```python
import jax
import jax.numpy as jnp
from jax import lax
from jax.experimental import pallas as pl
from jax.experimental.pallas import tpu as pltpu
from jax.sharding import PartitionSpec as P

STEP = 100
AXES = ("dp", "fsdp")

learn_rate = 0.01
galore_scale = 0.25

ROWS = 64
VMEM = 48 * 1024 * 1024


CORE, LO, X = 2, 2, 4
PAIR = 2 * ROWS


def pack_columns(place, tokens):
    count, width = tokens.shape
    steps = 4
    tall = count // steps

    def body(place_ref, x_ref, own_ref, send_ref):
        for now in range(2):

            @pl.when(place_ref[0] == now)
            def _():
                for j, (y, shard) in enumerate((y, shard) for y in range(4) for shard in range(LO * X)):
                    for out_ref, side in ((own_ref, now), (send_ref, 1 - now)):
                        a = shard * (width // (LO * X)) + y * 2 * PAIR + side * ROWS
                        out_ref[:, j * PAIR : (j + 1) * PAIR] = jnp.concatenate(
                            [x_ref[:, a : a + ROWS], x_ref[:, a + PAIR : a + PAIR + ROWS]], axis=1
                        )

    out = jax.ShapeDtypeStruct((count, width // 2), jnp.bfloat16)
    spec = pl.BlockSpec((tall, width // 2), lambda i, c: (i, 0))
    return pl.pallas_call(
        body,
        grid_spec=pltpu.PrefetchScalarGridSpec(
            num_scalar_prefetch=1,
            grid=(steps,),
            in_specs=[pl.BlockSpec((tall, width), lambda i, c: (i, 0))],
            out_specs=[spec, spec],
        ),
        out_shape=[out, out],
        compiler_params=pltpu.CompilerParams(vmem_limit_bytes=60 * 1024 * 1024),
        cost_estimate=pl.CostEstimate(flops=1, bytes_accessed=1, transcendentals=0),
        name="pack_columns",
    )(place, tokens)


def pack_rows(place, weight, after):
    chips, _, rows, features = weight.shape
    steps = 2
    block = chips // steps

    def body(place_ref, w_ref, after_ref, o_ref):
        o_ref[...] = w_ref[:, place_ref[0]]

    return pl.pallas_call(
        body,
        grid_spec=pltpu.PrefetchScalarGridSpec(
            num_scalar_prefetch=1,
            grid=(steps,),
            in_specs=[
                pl.BlockSpec((block, 2, rows, features), lambda i, c: (i, 0, 0, 0)),
                pl.BlockSpec(memory_space=pl.ANY),
            ],
            out_specs=pl.BlockSpec((block, rows, features), lambda i, c: (i, 0, 0)),
        ),
        out_shape=jax.ShapeDtypeStruct((chips, rows, features), weight.dtype),
        compiler_params=pltpu.CompilerParams(vmem_limit_bytes=VMEM),
        cost_estimate=pl.CostEstimate(flops=1, bytes_accessed=1, transcendentals=0),
        name="pack_rows",
    )(place, weight, after)


def keys_of(packed, shards, pieces):
    rows, features = pieces[0].shape
    count, many = len(pieces), len(packed)
    part = rows // 4
    tokens, depth = packed[0].shape
    wide = features // 4

    def body(shard_ref, *refs):
        ins, outs = refs[: many + count], refs[many + count : 2 * many + count]
        rows_ref, packed_ref, sems = refs[-3:]
        copies = [
            pltpu.make_async_copy(ins[many + k], rows_ref.at[:, shard_ref[k]], sems.at[many + k]) for k in range(count)
        ]
        copies = [pltpu.make_async_copy(ins[i], packed_ref.at[i], sems.at[i]) for i in range(many)] + copies
        for copy in copies:
            copy.start()
        for copy in copies:
            copy.wait()
        for i in range(many):
            for n in range(4):
                columns = slice(n * wide, (n + 1) * wide)
                block = rows_ref[:, :, :, columns].reshape(depth, wide)
                outs[i][:, columns] = jnp.dot(packed_ref[i], block, preferred_element_type=jnp.float32)

    return pl.pallas_call(
        body,
        grid_spec=pltpu.PrefetchScalarGridSpec(
            num_scalar_prefetch=1,
            grid=(),
            in_specs=[pl.BlockSpec(memory_space=pl.ANY)] * (many + count),
            out_specs=[pl.BlockSpec(memory_space=pltpu.VMEM)] * many,
            scratch_shapes=[
                pltpu.VMEM((4, count, part, features), jnp.bfloat16),
                pltpu.VMEM((many, tokens, depth), jnp.bfloat16),
                pltpu.SemaphoreType.DMA((many + count,)),
            ],
        ),
        out_shape=[jax.ShapeDtypeStruct((tokens, features), jnp.float32)] * many,
        compiler_params=pltpu.CompilerParams(vmem_limit_bytes=VMEM),
        cost_estimate=pl.CostEstimate(flops=1, bytes_accessed=1, transcendentals=0),
        name="keys_of",
    )(shards, *packed, *[piece.reshape(4, part, features) for piece in pieces])


def together(*arrays, after=()):
    def body(*refs):
        pass

    return pl.pallas_call(
        body,
        in_specs=[pl.BlockSpec(memory_space=pl.ANY)] * (len(arrays) + len(after)),
        out_specs=[pl.BlockSpec(memory_space=pl.ANY)] * len(arrays),
        out_shape=[jax.ShapeDtypeStruct(a.shape, a.dtype) for a in arrays],
        input_output_aliases={i: i for i in range(len(arrays))},
        name="together",
    )(*arrays, *after)


def device(x, y, z, core):
    return ((y % 4) * 4 + (z % 4 >> 1) * 2 + core % 2) * 8 + (z % 2) * 4 + x % 4


def every():
    return [(x, y, z, c) for y in range(4) for z in range(4) for c in range(2) for x in range(4)]


def move(array, x=0, y=0, z=0, core=0):
    return lax.ppermute(
        array, AXES, [(device(*at), device(at[0] + x, at[1] + y, at[2] + z, at[3] + core)) for at in every()]
    )


def move_apart(array, x=0, z=0):
    pairs = []
    for at in every():
        sign = 1 - 2 * at[3]
        pairs.append((device(*at), device(at[0] + sign * x, at[1], at[2] + sign * z, at[3])))
    return lax.ppermute(array, AXES, pairs)


def exchange(array, groups):
    return lax.all_to_all(array, AXES, split_axis=0, concat_axis=0, axis_index_groups=groups, tiled=True)


def local(tokens, cotangent, weight, basis, exp_avg, exp_avg_sq):
    core = lax.axis_index("dp") % 2
    shard = lax.axis_index("fsdp")
    my_x, my_lo = shard % X, shard // X
    my_z = lax.axis_index("dp") // 2 % 2 * 2 + my_lo
    features = weight.shape[1]
    chips = lax.axis_size("dp") // CORE
    rank = basis.shape[1]
    along_y = [[device(x, y, z, c) for y in range(4)] for x in range(4) for z in range(4) for c in range(2)]
    along_x = [[device(x, y, z, c) for x in range(4)] for y in range(4) for z in range(4) for c in range(2)]
    same_shard = [
        [device(x, y, z + 2 * hi, c) for y in range(4) for hi in range(2)]
        for x in range(4)
        for z in range(2)
        for c in range(2)
    ]
    place = core.reshape(1)

    def wide(array):
        return array.astype(jnp.float32)

    own, send = pack_columns(place, tokens)
    other = move(send, core=1)
    low = jnp.dot(cotangent, basis, preferred_element_type=jnp.float32).astype(jnp.bfloat16)
    low_other = move(low, core=1)

    half = pack_rows(place, weight.reshape(chips, CORE, ROWS, features), own).reshape(-1, features)
    w_up = move(half, x=-1)
    w_down = move(half, x=1)
    w_z = move_apart(half, z=-1)

    contract = (((0,), (0,)), ((), ()))
    partial = lax.dot_general(own, low, contract, preferred_element_type=jnp.float32)
    partial = partial + lax.dot_general(other, low_other, contract, preferred_element_type=jnp.float32)
    partial = partial.astype(jnp.bfloat16)

    def sum_all(spread):
        total = wide(spread[0])
        for i in range(1, spread.shape[0]):
            total = total + wide(spread[i])
        return total

    def take(parts, step):
        z = (my_z + step) % 4
        some = lax.dynamic_slice_in_dim(parts, z % 2, 1, axis=-5)
        some = lax.dynamic_slice_in_dim(some, z // 2, 1, axis=-3)
        return some.reshape(-1, ROWS, parts.shape[-1])

    def sum_z(own_part, others):
        total = wide(own_part)
        for step, part in others:
            total = total + wide(move(part, z=step))
        return total.astype(jnp.bfloat16)

    first = partial[:, : rank // 2].reshape(4, -1, rank // 2)
    first = sum_all(exchange(first, along_y)).astype(jnp.bfloat16)
    second = partial[:, rank // 2 :].reshape(4, LO, X, 2, ROWS, rank // 2)
    others = [(step, take(second, step)) for step in (1, 3, 2)]
    second = sum_z(take(second, 0), others)
    w_up, w_down, w_z = together(w_up, w_down, w_z, after=[part for _, part in others])
    zx_up = move(w_z, x=-1)
    zx_down = move(w_z, x=1)
    w_far = move_apart(jnp.where(core == 0, w_up, w_down), x=-1)
    second = sum_all(exchange(second.reshape(4, X * ROWS, rank // 2), along_y)).astype(jnp.bfloat16)
    first = first.reshape(LO, X, 2, ROWS, rank // 2)
    others = [(step, take(first, step)) for step in (1, 3, 2)]
    first = sum_z(take(first, 0), others)
    w_far, zx_up, zx_down = together(w_far, zx_up, zx_down, after=[part for _, part in others])
    zx_far = move_apart(w_far, z=-1)
    both = jnp.concatenate([first.reshape(X, ROWS, -1), second.reshape(X, ROWS, -1)], axis=2)
    projected = sum_all(exchange(both, along_x))
    new_avg = 0.9 * exp_avg + 0.1 * projected
    new_sq = 0.999 * exp_avg_sq + 0.001 * projected * projected
    first_fix = 1.0 - 0.9**STEP
    second_fix = 1.0 - 0.999**STEP
    direction = new_avg / first_fix / (jnp.sqrt(new_sq / second_fix) + 1e-08)
    direction = direction.astype(jnp.bfloat16)
    (zx_far,) = together(zx_far, after=(direction,))
    steps = [(0, 0), (0, 1), (0, 3), (1, 0), (1, 1), (1, 3), (0, 2), (1, 2)]
    shards = jnp.stack([(my_lo + lo) % LO * X + (my_x + x) % X for lo, x in steps])
    for_other, own_keys = keys_of([other, own], shards, [half, w_up, w_down, w_z, zx_up, zx_down, w_far, zx_far])
    mine = exchange(jnp.broadcast_to(direction[None], (chips, ROWS, rank)), same_shard)
    theirs = move(mine, core=1)
    (for_other,) = together(for_other, after=(mine,))
    keys = (own_keys + move(for_other, core=1)).astype(jnp.bfloat16)
    even = jnp.where(core == 0, mine, theirs)
    odd = jnp.where(core == 0, theirs, mine)
    update = lax.dot_general(
        jnp.stack([even, odd], axis=1).reshape(-1, rank),
        basis,
        (((1,), (1,)), ((), ())),
        preferred_element_type=jnp.float32,
    )
    new_weight = (wide(weight) - learn_rate * galore_scale * update).astype(jnp.bfloat16)
    return (keys, new_weight, new_avg, new_sq)


def solution(mesh):
    in_specs = (
        P(("dp", "fsdp"), None),
        P(("dp", "fsdp"), None),
        P("fsdp", None),
        P(),
        P(("fsdp", "dp"), None),
        P(("fsdp", "dp"), None),
    )
    out_specs = (
        P(("dp", "fsdp"), None),
        P("fsdp", None),
        P(("fsdp", "dp"), None),
        P(("fsdp", "dp"), None),
    )
    return jax.shard_map(local, mesh=mesh, in_specs=in_specs, out_specs=out_specs, check_vma=False)
```

```python
import jax
import jax.numpy as jnp
from jax import lax
from jax.experimental import pallas as pl
from jax.experimental.pallas import tpu as pltpu
from jax.sharding import PartitionSpec as P

STEP = 100
AXES = ("dp", "fsdp")

learn_rate = 0.01
galore_scale = 0.25

ROWS = 64
VMEM = 60 * 1024 * 1024


CORE, LO, X = 2, 2, 4
PAIR = 2 * ROWS


def pack_columns(place, tokens):
    count, width = tokens.shape
    steps = 4
    tall = count // steps

    def body(place_ref, x_ref, own_ref, send_ref):
        for now in range(2):

            @pl.when(place_ref[0] == now)
            def _():
                for j, (y, shard) in enumerate((y, shard) for y in range(4) for shard in range(LO * X)):
                    for out_ref, side in ((own_ref, now), (send_ref, 1 - now)):
                        a = shard * (width // (LO * X)) + y * 2 * PAIR + side * ROWS
                        out_ref[:, j * PAIR : (j + 1) * PAIR] = jnp.concatenate(
                            [x_ref[:, a : a + ROWS], x_ref[:, a + PAIR : a + PAIR + ROWS]], axis=1
                        )

    out = jax.ShapeDtypeStruct((count, width // 2), jnp.bfloat16)
    spec = pl.BlockSpec((tall, width // 2), lambda i, c: (i, 0))
    return pl.pallas_call(
        body,
        grid_spec=pltpu.PrefetchScalarGridSpec(
            num_scalar_prefetch=1,
            grid=(steps,),
            in_specs=[pl.BlockSpec((tall, width), lambda i, c: (i, 0))],
            out_specs=[spec, spec],
        ),
        out_shape=[out, out],
        compiler_params=pltpu.CompilerParams(vmem_limit_bytes=VMEM),
        cost_estimate=pl.CostEstimate(flops=1, bytes_accessed=1, transcendentals=0),
        name="pack_columns",
    )(place, tokens)


def pack_rows(place, weight, after):
    chips, _, rows, features = weight.shape
    steps = 2
    block = chips // steps

    def body(place_ref, w_ref, after_ref, o_ref):
        o_ref[...] = w_ref[:, place_ref[0]]

    return pl.pallas_call(
        body,
        grid_spec=pltpu.PrefetchScalarGridSpec(
            num_scalar_prefetch=1,
            grid=(steps,),
            in_specs=[
                pl.BlockSpec((block, 2, rows, features), lambda i, c: (i, 0, 0, 0)),
                pl.BlockSpec(memory_space=pl.ANY),
            ],
            out_specs=pl.BlockSpec((block, rows, features), lambda i, c: (i, 0, 0)),
        ),
        out_shape=jax.ShapeDtypeStruct((chips, rows, features), weight.dtype),
        compiler_params=pltpu.CompilerParams(vmem_limit_bytes=VMEM),
        cost_estimate=pl.CostEstimate(flops=1, bytes_accessed=1, transcendentals=0),
        name="pack_rows",
    )(place, weight, after)


def keys_of(packed, shards, pieces, addends=(), after=()):
    rows, features = pieces[0].shape
    count, many = len(pieces), len(packed)
    part = rows // 4
    tokens, width = packed[0].shape
    every_shard = width // rows
    depth = count * rows
    wide = features // 4
    inputs = many + count + len(addends) + len(after)

    def body(shard_ref, *refs):
        ins, plus, outs = refs[: many + count], refs[many + count :], refs[inputs : inputs + many]
        rows_ref, packed_ref, sems = refs[-3:]
        copies = [pltpu.make_async_copy(ins[many + k], rows_ref.at[:, k], sems.at[many, k]) for k in range(count)]
        loads = []
        for i in range(many):
            loads.append([])
            for y in range(4):
                for k in range(count):
                    at = pl.multiple_of((y * every_shard + shard_ref[k]) * part, part)
                    to = packed_ref.at[i, :, pl.ds((y * count + k) * part, part)]
                    loads[i].append(pltpu.make_async_copy(ins[i].at[:, pl.ds(at, part)], to, sems.at[i, y * count + k]))
        for copy in copies + sum(loads, []):
            copy.start()
        for copy in copies:
            copy.wait()
        for i in range(many):
            for copy in loads[i]:
                copy.wait()
            for n in range(4):
                columns = slice(n * wide, (n + 1) * wide)
                block = rows_ref[:, :, :, columns].reshape(depth, wide)
                product = jnp.dot(packed_ref[i], block, preferred_element_type=jnp.float32)
                outs[i][:, columns] = product + plus[i][:, columns] if addends else product

    return pl.pallas_call(
        body,
        grid_spec=pltpu.PrefetchScalarGridSpec(
            num_scalar_prefetch=1,
            grid=(),
            in_specs=[pl.BlockSpec(memory_space=pl.ANY)] * (many + count)
            + [pl.BlockSpec(memory_space=pltpu.VMEM)] * len(addends)
            + [pl.BlockSpec(memory_space=pl.ANY)] * len(after),
            out_specs=[pl.BlockSpec(memory_space=pltpu.VMEM)] * many,
            scratch_shapes=[
                pltpu.VMEM((4, count, part, features), jnp.bfloat16),
                pltpu.VMEM((many, tokens, depth), jnp.bfloat16),
                pltpu.SemaphoreType.DMA((many + 1, 4 * count)),
            ],
        ),
        out_shape=[jax.ShapeDtypeStruct((tokens, features), jnp.float32)] * many,
        compiler_params=pltpu.CompilerParams(vmem_limit_bytes=VMEM),
        cost_estimate=pl.CostEstimate(
            flops=1 if addends else 2 * many * tokens * depth * features,
            bytes_accessed=1 if addends else 2 * depth * (many * tokens + features),
            transcendentals=0,
        ),
        name="keys_of",
    )(shards, *packed, *[piece.reshape(4, part, features) for piece in pieces], *addends, *after)


def together(*arrays, after=()):
    def body(*refs):
        pass

    return pl.pallas_call(
        body,
        in_specs=[pl.BlockSpec(memory_space=pl.ANY)] * (len(arrays) + len(after)),
        out_specs=[pl.BlockSpec(memory_space=pl.ANY)] * len(arrays),
        out_shape=[jax.ShapeDtypeStruct(a.shape, a.dtype) for a in arrays],
        input_output_aliases={i: i for i in range(len(arrays))},
        name="together",
    )(*arrays, *after)


def device(x, y, z, core):
    return ((y % 4) * 4 + (z % 4 >> 1) * 2 + core % 2) * 8 + (z % 2) * 4 + x % 4


def every():
    return [(x, y, z, c) for y in range(4) for z in range(4) for c in range(2) for x in range(4)]


def move(array, x=0, y=0, z=0, core=0):
    return lax.ppermute(
        array, AXES, [(device(*at), device(at[0] + x, at[1] + y, at[2] + z, at[3] + core)) for at in every()]
    )


def move_apart(array, x=0, z=0):
    pairs = []
    for at in every():
        sign = 1 - 2 * at[3]
        pairs.append((device(*at), device(at[0] + sign * x, at[1], at[2] + sign * z, at[3])))
    return lax.ppermute(array, AXES, pairs)


def exchange(array, groups):
    return lax.all_to_all(array, AXES, split_axis=0, concat_axis=0, axis_index_groups=groups, tiled=True)


def local(tokens, cotangent, weight, basis, exp_avg, exp_avg_sq):
    core = lax.axis_index("dp") % 2
    shard = lax.axis_index("fsdp")
    my_x, my_lo = shard % X, shard // X
    my_z = lax.axis_index("dp") // 2 % 2 * 2 + my_lo
    features = weight.shape[1]
    chips = lax.axis_size("dp") // CORE
    rank = basis.shape[1]
    along_y = [[device(x, y, z, c) for y in range(4)] for x in range(4) for z in range(4) for c in range(2)]
    along_x = [[device(x, y, z, c) for x in range(4)] for y in range(4) for z in range(4) for c in range(2)]
    same_shard = [
        [device(x, y, z + 2 * hi, c) for y in range(4) for hi in range(2)]
        for x in range(4)
        for z in range(2)
        for c in range(2)
    ]
    place = core.reshape(1)

    def wide(array):
        return array.astype(jnp.float32)

    own, send = pack_columns(place, tokens)
    other = move(send, core=1)
    low = jnp.dot(cotangent, basis, preferred_element_type=jnp.float32).astype(jnp.bfloat16)
    low_other = move(low, core=1)

    half = pack_rows(place, weight.reshape(chips, CORE, ROWS, features), own).reshape(-1, features)
    w_up = move(half, x=-1)
    w_down = move(half, x=1)
    w_z = move_apart(half, z=-1)

    contract = (((0,), (0,)), ((), ()))
    partial = lax.dot_general(own, low, contract, preferred_element_type=jnp.float32)
    partial = partial + lax.dot_general(other, low_other, contract, preferred_element_type=jnp.float32)
    partial = partial.astype(jnp.bfloat16)

    def sum_all(spread):
        total = wide(spread[0])
        for i in range(1, spread.shape[0]):
            total = total + wide(spread[i])
        return total

    def take(parts, step):
        z = (my_z + step) % 4
        some = lax.dynamic_slice_in_dim(parts, z % 2, 1, axis=-5)
        some = lax.dynamic_slice_in_dim(some, z // 2, 1, axis=-3)
        return some.reshape(-1, ROWS, parts.shape[-1])

    def sum_z(own_part, others):
        total = wide(own_part)
        for step, part in others:
            total = total + wide(move(part, z=step))
        return total.astype(jnp.bfloat16)

    first = partial[:, : rank // 2].reshape(4, -1, rank // 2)
    first = sum_all(exchange(first, along_y)).astype(jnp.bfloat16)
    second = partial[:, rank // 2 :].reshape(4, LO, X, 2, ROWS, rank // 2)
    others = [(step, take(second, step)) for step in (1, 3, 2)]
    second = sum_z(take(second, 0), others)
    w_up, w_down, w_z = together(w_up, w_down, w_z, after=[part for _, part in others])
    zx_up = move(w_z, x=-1)
    zx_down = move(w_z, x=1)
    steps = [(0, 0), (0, 1), (0, 3), (1, 0), (1, 1), (1, 3), (0, 2), (1, 2)]
    shards = jnp.stack([(my_lo + lo) % LO * X + (my_x + x) % X for lo, x in steps])
    other_near, own_near = keys_of([other, own], shards[:4], [half, w_up, w_down, w_z])
    second, w_far = together(second, jnp.where(core == 0, w_up, w_down), after=(own_near,))
    w_far = move_apart(w_far, x=-1)
    second = sum_all(exchange(second.reshape(4, X * ROWS, rank // 2), along_y)).astype(jnp.bfloat16)
    first = first.reshape(LO, X, 2, ROWS, rank // 2)
    others = [(step, take(first, step)) for step in (1, 3, 2)]
    first = sum_z(take(first, 0), others)
    w_far, zx_up, zx_down = together(w_far, zx_up, zx_down, after=[part for _, part in others])
    zx_far = move_apart(w_far, z=-1)
    both = jnp.concatenate([first.reshape(X, ROWS, -1), second.reshape(X, ROWS, -1)], axis=2)
    projected = sum_all(exchange(both, along_x))
    new_avg = 0.9 * exp_avg + 0.1 * projected
    new_sq = 0.999 * exp_avg_sq + 0.001 * projected * projected
    first_fix = 1.0 - 0.9**STEP
    second_fix = 1.0 - 0.999**STEP
    direction = new_avg / first_fix / (jnp.sqrt(new_sq / second_fix) + 1e-08)
    direction = direction.astype(jnp.bfloat16)
    for_other, own_keys = keys_of(
        [other, own], shards[4:], [zx_up, zx_down, w_far, zx_far], [other_near, own_near], (direction,)
    )

    mine = exchange(jnp.broadcast_to(direction[None], (chips, ROWS, rank)), same_shard)
    theirs = move(mine, core=1)
    (for_other,) = together(for_other, after=(mine,))
    keys = (own_keys + move(for_other, core=1)).astype(jnp.bfloat16)
    even = jnp.where(core == 0, mine, theirs)
    odd = jnp.where(core == 0, theirs, mine)
    update = lax.dot_general(
        jnp.stack([even, odd], axis=1).reshape(-1, rank),
        basis,
        (((1,), (1,)), ((), ())),
        preferred_element_type=jnp.float32,
    )
    new_weight = (wide(weight) - learn_rate * galore_scale * update).astype(jnp.bfloat16)
    return (keys, new_weight, new_avg, new_sq)


def solution(mesh):
    in_specs = (
        P(("dp", "fsdp"), None),
        P(("dp", "fsdp"), None),
        P("fsdp", None),
        P(),
        P(("fsdp", "dp"), None),
        P(("fsdp", "dp"), None),
    )
    out_specs = (
        P(("dp", "fsdp"), None),
        P("fsdp", None),
        P(("fsdp", "dp"), None),
        P(("fsdp", "dp"), None),
    )
    return jax.shard_map(local, mesh=mesh, in_specs=in_specs, out_specs=out_specs, check_vma=False)
```

```python
import jax
import jax.numpy as jnp
from jax import lax
from jax.experimental import pallas as pl
from jax.experimental.pallas import tpu as pltpu
from jax.sharding import PartitionSpec as P

STEP = 100
AXES = ("dp", "fsdp")

learn_rate = 0.01
galore_scale = 0.25

ROWS = 64
VMEM = 60 * 1024 * 1024


CORE, LO, X = 2, 2, 4
PAIR = 2 * ROWS


def pack_columns(place, tokens):
    count, width = tokens.shape
    steps = 4
    tall = count // steps

    def body(place_ref, x_ref, own_ref, send_ref):
        for now in range(2):

            @pl.when(place_ref[0] == now)
            def _():
                for j, (y, shard) in enumerate((y, shard) for y in range(4) for shard in range(LO * X)):
                    for out_ref, side in ((own_ref, now), (send_ref, 1 - now)):
                        a = shard * (width // (LO * X)) + y * 2 * PAIR + side * ROWS
                        out_ref[:, j * PAIR : (j + 1) * PAIR] = jnp.concatenate(
                            [x_ref[:, a : a + ROWS], x_ref[:, a + PAIR : a + PAIR + ROWS]], axis=1
                        )

    out = jax.ShapeDtypeStruct((count, width // 2), jnp.bfloat16)
    spec = pl.BlockSpec((tall, width // 2), lambda i, c: (i, 0))
    return pl.pallas_call(
        body,
        grid_spec=pltpu.PrefetchScalarGridSpec(
            num_scalar_prefetch=1,
            grid=(steps,),
            in_specs=[pl.BlockSpec((tall, width), lambda i, c: (i, 0))],
            out_specs=[spec, spec],
        ),
        out_shape=[out, out],
        compiler_params=pltpu.CompilerParams(vmem_limit_bytes=VMEM),
        cost_estimate=pl.CostEstimate(flops=1, bytes_accessed=1, transcendentals=0),
        name="pack_columns",
    )(place, tokens)


def pack_rows(place, weight, after):
    chips, _, rows, features = weight.shape
    steps = 2
    block = chips // steps

    def body(place_ref, w_ref, after_ref, o_ref):
        o_ref[...] = w_ref[:, place_ref[0]]

    return pl.pallas_call(
        body,
        grid_spec=pltpu.PrefetchScalarGridSpec(
            num_scalar_prefetch=1,
            grid=(steps,),
            in_specs=[
                pl.BlockSpec((block, 2, rows, features), lambda i, c: (i, 0, 0, 0)),
                pl.BlockSpec(memory_space=pl.ANY),
            ],
            out_specs=pl.BlockSpec((block, rows, features), lambda i, c: (i, 0, 0)),
        ),
        out_shape=jax.ShapeDtypeStruct((chips, rows, features), weight.dtype),
        compiler_params=pltpu.CompilerParams(vmem_limit_bytes=VMEM),
        cost_estimate=pl.CostEstimate(flops=1, bytes_accessed=1, transcendentals=0),
        name="pack_rows",
    )(place, weight, after)


def keys_of(packed, shard, steps, pieces, addends=(), after=()):
    rows, features = pieces[0].shape
    count, many = len(pieces), len(packed)
    part = rows // 4
    tokens, width = packed[0].shape
    every_shard = width // rows
    depth = count * rows
    wide = features // 4
    inputs = many + count + len(addends) + len(after)

    def body(shard_ref, *refs):
        ins, plus, outs = refs[: many + count], refs[many + count :], refs[inputs : inputs + many]
        rows_ref, packed_ref, sems = refs[-3:]
        at_lo, at_x = shard_ref[0] // X, shard_ref[0] % X
        shards = [(at_lo + lo) % LO * X + (at_x + x) % X for lo, x in steps]
        copies = [pltpu.make_async_copy(ins[many + k], rows_ref.at[:, k], sems.at[many, k]) for k in range(count)]
        loads = []
        for i in range(many):
            loads.append([])
            for y in range(4):
                for k in range(count):
                    at = pl.multiple_of((y * every_shard + shards[k]) * part, part)
                    to = packed_ref.at[i, :, pl.ds((y * count + k) * part, part)]
                    loads[i].append(pltpu.make_async_copy(ins[i].at[:, pl.ds(at, part)], to, sems.at[i, y * count + k]))
        for copy in copies + sum(loads, []):
            copy.start()
        for copy in copies:
            copy.wait()
        for i in range(many):
            for copy in loads[i]:
                copy.wait()
            for n in range(4):
                columns = slice(n * wide, (n + 1) * wide)
                block = rows_ref[:, :, :, columns].reshape(depth, wide)
                product = jnp.dot(packed_ref[i], block, preferred_element_type=jnp.float32)
                outs[i][:, columns] = product + plus[i][:, columns] if addends else product

    return pl.pallas_call(
        body,
        grid_spec=pltpu.PrefetchScalarGridSpec(
            num_scalar_prefetch=1,
            grid=(),
            in_specs=[pl.BlockSpec(memory_space=pl.ANY)] * (many + count)
            + [pl.BlockSpec(memory_space=pltpu.VMEM)] * len(addends)
            + [pl.BlockSpec(memory_space=pl.ANY)] * len(after),
            out_specs=[pl.BlockSpec(memory_space=pltpu.VMEM)] * many,
            scratch_shapes=[
                pltpu.VMEM((4, count, part, features), jnp.bfloat16),
                pltpu.VMEM((many, tokens, depth), jnp.bfloat16),
                pltpu.SemaphoreType.DMA((many + 1, 4 * count)),
            ],
        ),
        out_shape=[jax.ShapeDtypeStruct((tokens, features), jnp.float32)] * many,
        compiler_params=pltpu.CompilerParams(vmem_limit_bytes=VMEM),
        cost_estimate=pl.CostEstimate(
            flops=1 if addends else 2 * many * tokens * depth * features,
            bytes_accessed=1 if addends else 2 * depth * (many * tokens + features),
            transcendentals=0,
        ),
        name="keys_of",
    )(shard, *packed, *[piece.reshape(4, part, features) for piece in pieces], *addends, *after)


def together(*arrays, after=()):
    def body(*refs):
        pass

    return pl.pallas_call(
        body,
        in_specs=[pl.BlockSpec(memory_space=pl.ANY)] * (len(arrays) + len(after)),
        out_specs=[pl.BlockSpec(memory_space=pl.ANY)] * len(arrays),
        out_shape=[jax.ShapeDtypeStruct(a.shape, a.dtype) for a in arrays],
        input_output_aliases={i: i for i in range(len(arrays))},
        name="together",
    )(*arrays, *after)


def device(x, y, z, core):
    return ((y % 4) * 4 + (z % 4 >> 1) * 2 + core % 2) * 8 + (z % 2) * 4 + x % 4


def every():
    return [(x, y, z, c) for y in range(4) for z in range(4) for c in range(2) for x in range(4)]


def move(array, x=0, y=0, z=0, core=0):
    return lax.ppermute(
        array, AXES, [(device(*at), device(at[0] + x, at[1] + y, at[2] + z, at[3] + core)) for at in every()]
    )


def move_apart(array, x=0, z=0):
    pairs = []
    for at in every():
        sign = 1 - 2 * at[3]
        pairs.append((device(*at), device(at[0] + sign * x, at[1], at[2] + sign * z, at[3])))
    return lax.ppermute(array, AXES, pairs)


def exchange(array, groups):
    return lax.all_to_all(array, AXES, split_axis=0, concat_axis=0, axis_index_groups=groups, tiled=True)


def local(tokens, cotangent, weight, basis, exp_avg, exp_avg_sq):
    core = lax.axis_index("dp") % 2
    shard = lax.axis_index("fsdp")
    my_lo = shard // X
    my_z = lax.axis_index("dp") // 2 % 2 * 2 + my_lo
    features = weight.shape[1]
    chips = lax.axis_size("dp") // CORE
    rank = basis.shape[1]
    along_y = [[device(x, y, z, c) for y in range(4)] for x in range(4) for z in range(4) for c in range(2)]
    along_x = [[device(x, y, z, c) for x in range(4)] for y in range(4) for z in range(4) for c in range(2)]
    same_shard = [
        [device(x, y, z + 2 * hi, c) for y in range(4) for hi in range(2)]
        for x in range(4)
        for z in range(2)
        for c in range(2)
    ]
    place = core.reshape(1)

    def wide(array):
        return array.astype(jnp.float32)

    own, send = pack_columns(place, tokens)
    other = move(send, core=1)
    low = jnp.dot(cotangent, basis, preferred_element_type=jnp.float32).astype(jnp.bfloat16)
    low_other = move(low, core=1)

    half = pack_rows(place, weight.reshape(chips, CORE, ROWS, features), own).reshape(-1, features)
    w_up = move(half, x=-1)
    w_down = move(half, x=1)
    w_z = move_apart(half, z=-1)

    contract = (((0,), (0,)), ((), ()))
    partial = lax.dot_general(own, low, contract, preferred_element_type=jnp.float32)
    partial = partial + lax.dot_general(other, low_other, contract, preferred_element_type=jnp.float32)
    partial = partial.astype(jnp.bfloat16)

    def sum_all(spread):
        total = wide(spread[0])
        for i in range(1, spread.shape[0]):
            total = total + wide(spread[i])
        return total

    def take(parts, step):
        z = (my_z + step) % 4
        some = lax.dynamic_slice_in_dim(parts, z % 2, 1, axis=-5)
        some = lax.dynamic_slice_in_dim(some, z // 2, 1, axis=-3)
        return some.reshape(-1, ROWS, parts.shape[-1])

    def sum_z(own_part, others):
        total = wide(own_part)
        for step, part in others:
            total = total + wide(move(part, z=step))
        return total.astype(jnp.bfloat16)

    first = partial[:, : rank // 2].reshape(4, -1, rank // 2)
    first = sum_all(exchange(first, along_y)).astype(jnp.bfloat16)
    second = partial[:, rank // 2 :].reshape(4, LO, X, 2, ROWS, rank // 2)
    others = [(step, take(second, step)) for step in (1, 3, 2)]
    second = sum_z(take(second, 0), others)
    w_up, w_down, w_z = together(w_up, w_down, w_z, after=[part for _, part in others])
    zx_up = move(w_z, x=-1)
    zx_down = move(w_z, x=1)
    steps = [(0, 0), (0, 1), (0, 3), (1, 0), (1, 1), (1, 3), (0, 2), (1, 2)]
    at = shard.reshape(1)
    other_near, own_near = keys_of([other, own], at, steps[:4], [half, w_up, w_down, w_z])
    second, w_far = together(second, jnp.where(core == 0, w_up, w_down), after=(own_near,))
    w_far = move_apart(w_far, x=-1)
    second = sum_all(exchange(second.reshape(4, X * ROWS, rank // 2), along_y)).astype(jnp.bfloat16)
    first = first.reshape(LO, X, 2, ROWS, rank // 2)
    others = [(step, take(first, step)) for step in (1, 3, 2)]
    first = sum_z(take(first, 0), others)
    w_far, zx_up, zx_down = together(w_far, zx_up, zx_down, after=[part for _, part in others])
    zx_far = move_apart(w_far, z=-1)
    both = jnp.concatenate([first.reshape(X, ROWS, -1), second.reshape(X, ROWS, -1)], axis=2)
    projected = sum_all(exchange(both, along_x))
    new_avg = 0.9 * exp_avg + 0.1 * projected
    new_sq = 0.999 * exp_avg_sq + 0.001 * projected * projected
    first_fix = 1.0 - 0.9**STEP
    second_fix = 1.0 - 0.999**STEP
    direction = new_avg / first_fix / (jnp.sqrt(new_sq / second_fix) + 1e-08)
    direction = direction.astype(jnp.bfloat16)
    for_other, own_keys = keys_of(
        [other, own], at, steps[4:], [zx_up, zx_down, w_far, zx_far], [other_near, own_near], (direction,)
    )

    mine = exchange(jnp.broadcast_to(direction[None], (chips, ROWS, rank)), same_shard)
    theirs = move(mine, core=1)
    (for_other,) = together(for_other, after=(mine,))
    keys = (own_keys + move(for_other, core=1)).astype(jnp.bfloat16)
    even = jnp.where(core == 0, mine, theirs)
    odd = jnp.where(core == 0, theirs, mine)
    update = lax.dot_general(
        jnp.stack([even, odd], axis=1).reshape(-1, rank),
        basis,
        (((1,), (1,)), ((), ())),
        preferred_element_type=jnp.float32,
    )
    new_weight = (wide(weight) - learn_rate * galore_scale * update).astype(jnp.bfloat16)
    return (keys, new_weight, new_avg, new_sq)


def solution(mesh):
    in_specs = (
        P(("dp", "fsdp"), None),
        P(("dp", "fsdp"), None),
        P("fsdp", None),
        P(),
        P(("fsdp", "dp"), None),
        P(("fsdp", "dp"), None),
    )
    out_specs = (
        P(("dp", "fsdp"), None),
        P("fsdp", None),
        P(("fsdp", "dp"), None),
        P(("fsdp", "dp"), None),
    )
    return jax.shard_map(local, mesh=mesh, in_specs=in_specs, out_specs=out_specs, check_vma=False)
```

```python
import jax
import jax.numpy as jnp
from jax import lax
from jax.experimental import pallas as pl
from jax.experimental.pallas import tpu as pltpu
from jax.sharding import PartitionSpec as P

STEP = 100
AXES = ("dp", "fsdp")

learn_rate = 0.01
galore_scale = 0.25

ROWS = 64
VMEM = 60 * 1024 * 1024


CORE, LO, X = 2, 2, 4
PAIR = 2 * ROWS


def pack_columns(place, tokens):
    count, width = tokens.shape
    steps = 4
    tall = count // steps

    def body(place_ref, x_ref, own_ref, send_ref):
        for now in range(2):

            @pl.when(place_ref[0] == now)
            def _():
                for j, (y, shard) in enumerate((y, shard) for y in range(4) for shard in range(LO * X)):
                    for out_ref, side in ((own_ref, now), (send_ref, 1 - now)):
                        a = shard * (width // (LO * X)) + y * 2 * PAIR + side * ROWS
                        out_ref[:, j * PAIR : (j + 1) * PAIR] = jnp.concatenate(
                            [x_ref[:, a : a + ROWS], x_ref[:, a + PAIR : a + PAIR + ROWS]], axis=1
                        )

    out = jax.ShapeDtypeStruct((count, width // 2), jnp.bfloat16)
    spec = pl.BlockSpec((tall, width // 2), lambda i, c: (i, 0))
    return pl.pallas_call(
        body,
        grid_spec=pltpu.PrefetchScalarGridSpec(
            num_scalar_prefetch=1,
            grid=(steps,),
            in_specs=[pl.BlockSpec((tall, width), lambda i, c: (i, 0))],
            out_specs=[spec, spec],
        ),
        out_shape=[out, out],
        compiler_params=pltpu.CompilerParams(vmem_limit_bytes=VMEM),
        cost_estimate=pl.CostEstimate(flops=1, bytes_accessed=1, transcendentals=0),
        name="pack_columns",
    )(place, tokens)


def pack_rows(place, weight, after):
    chips, _, rows, features = weight.shape
    steps = 2
    block = chips // steps

    def body(place_ref, w_ref, after_ref, o_ref):
        o_ref[...] = w_ref[:, place_ref[0]]

    return pl.pallas_call(
        body,
        grid_spec=pltpu.PrefetchScalarGridSpec(
            num_scalar_prefetch=1,
            grid=(steps,),
            in_specs=[
                pl.BlockSpec((block, 2, rows, features), lambda i, c: (i, 0, 0, 0)),
                pl.BlockSpec(memory_space=pl.ANY),
            ],
            out_specs=pl.BlockSpec((block, rows, features), lambda i, c: (i, 0, 0)),
        ),
        out_shape=jax.ShapeDtypeStruct((chips, rows, features), weight.dtype),
        compiler_params=pltpu.CompilerParams(vmem_limit_bytes=VMEM),
        cost_estimate=pl.CostEstimate(flops=1, bytes_accessed=1, transcendentals=0),
        name="pack_rows",
    )(place, weight, after)


def keys_of(packed, shard, steps, pieces, addends=(), after=()):
    rows, features = pieces[0].shape
    count, many = len(pieces), len(packed)
    part = rows // 4
    tokens, width = packed[0].shape
    every_shard = width // rows
    depth = count * rows
    wide = features // 4
    inputs = many + count + len(addends) + len(after)

    def body(shard_ref, *refs):
        ins, plus, outs = refs[: many + count], refs[many + count :], refs[inputs : inputs + many]
        rows_ref, packed_ref, sems = refs[-3:]
        at_lo, at_x = shard_ref[0] // X, shard_ref[0] % X
        shards = [(at_lo + lo) % LO * X + (at_x + x) % X for lo, x in steps]
        copies = [pltpu.make_async_copy(ins[many + k], rows_ref.at[:, k], sems.at[many, k]) for k in range(count)]
        loads = []
        for i in range(many):
            loads.append([])
            for y in range(4):
                for k in range(count):
                    at = pl.multiple_of((y * every_shard + shards[k]) * part, part)
                    to = packed_ref.at[i, :, pl.ds((y * count + k) * part, part)]
                    loads[i].append(pltpu.make_async_copy(ins[i].at[:, pl.ds(at, part)], to, sems.at[i, y * count + k]))
        for copy in copies + sum(loads, []):
            copy.start()
        for copy in copies:
            copy.wait()
        for i in range(many):
            for copy in loads[i]:
                copy.wait()
            for n in range(4):
                columns = slice(n * wide, (n + 1) * wide)
                block = rows_ref[:, :, :, columns].reshape(depth, wide)
                product = jnp.dot(packed_ref[i], block, preferred_element_type=jnp.float32)
                outs[i][:, columns] = product + plus[i][:, columns] if addends else product

    return pl.pallas_call(
        body,
        grid_spec=pltpu.PrefetchScalarGridSpec(
            num_scalar_prefetch=1,
            grid=(),
            in_specs=[pl.BlockSpec(memory_space=pl.ANY)] * (many + count)
            + [pl.BlockSpec(memory_space=pltpu.VMEM)] * len(addends)
            + [pl.BlockSpec(memory_space=pl.ANY)] * len(after),
            out_specs=[pl.BlockSpec(memory_space=pltpu.VMEM)] * many,
            scratch_shapes=[
                pltpu.VMEM((4, count, part, features), jnp.bfloat16),
                pltpu.VMEM((many, tokens, depth), jnp.bfloat16),
                pltpu.SemaphoreType.DMA((many + 1, 4 * count)),
            ],
        ),
        out_shape=[jax.ShapeDtypeStruct((tokens, features), jnp.float32)] * many,
        compiler_params=pltpu.CompilerParams(vmem_limit_bytes=VMEM),
        cost_estimate=pl.CostEstimate(
            flops=1 if addends else 2 * many * tokens * depth * features,
            bytes_accessed=1 if addends else 2 * depth * (many * tokens + features),
            transcendentals=0,
        ),
        name="keys_of",
    )(shard, *packed, *[piece.reshape(4, part, features) for piece in pieces], *addends, *after)


def together(*arrays, after=()):
    def body(*refs):
        pass

    return pl.pallas_call(
        body,
        in_specs=[pl.BlockSpec(memory_space=pl.ANY)] * (len(arrays) + len(after)),
        out_specs=[pl.BlockSpec(memory_space=pl.ANY)] * len(arrays),
        out_shape=[jax.ShapeDtypeStruct(a.shape, a.dtype) for a in arrays],
        input_output_aliases={i: i for i in range(len(arrays))},
        name="together",
    )(*arrays, *after)


def device(x, y, z, core):
    return ((y % 4) * 4 + (z % 4 >> 1) * 2 + core % 2) * 8 + (z % 2) * 4 + x % 4


def every():
    return [(x, y, z, c) for y in range(4) for z in range(4) for c in range(2) for x in range(4)]


def move(array, x=0, y=0, z=0, core=0):
    return lax.ppermute(
        array, AXES, [(device(*at), device(at[0] + x, at[1] + y, at[2] + z, at[3] + core)) for at in every()]
    )


def move_apart(array, x=0, z=0):
    pairs = []
    for at in every():
        sign = 1 - 2 * at[3]
        pairs.append((device(*at), device(at[0] + sign * x, at[1], at[2] + sign * z, at[3])))
    return lax.ppermute(array, AXES, pairs)


def exchange(array, groups):
    return lax.all_to_all(array, AXES, split_axis=0, concat_axis=0, axis_index_groups=groups, tiled=True)


def local(tokens, cotangent, weight, basis, exp_avg, exp_avg_sq):
    core = lax.axis_index("dp") % 2
    shard = lax.axis_index("fsdp")
    my_lo = shard // X
    my_z = lax.axis_index("dp") // 2 % 2 * 2 + my_lo
    features = weight.shape[1]
    chips = lax.axis_size("dp") // CORE
    rank = basis.shape[1]
    along_y = [[device(x, y, z, c) for y in range(4)] for x in range(4) for z in range(4) for c in range(2)]
    along_x = [[device(x, y, z, c) for x in range(4)] for y in range(4) for z in range(4) for c in range(2)]
    same_shard = [
        [device(x, y, z + 2 * hi, c) for y in range(4) for hi in range(2)]
        for x in range(4)
        for z in range(2)
        for c in range(2)
    ]
    place = core.reshape(1)

    def wide(array):
        return array.astype(jnp.float32)

    own, send = pack_columns(place, tokens)
    other = move(send, core=1)
    low = jnp.dot(cotangent, basis, preferred_element_type=jnp.float32).astype(jnp.bfloat16)
    low_other = move(low, core=1)

    half = pack_rows(place, weight.reshape(chips, CORE, ROWS, features), own).reshape(-1, features)
    w_up = move(half, x=-1)
    w_down = move(half, x=1)
    w_z = move_apart(half, z=-1)

    contract = (((0,), (0,)), ((), ()))
    partial = lax.dot_general(own, low, contract, preferred_element_type=jnp.float32)
    partial = partial + lax.dot_general(other, low_other, contract, preferred_element_type=jnp.float32)
    partial = partial.astype(jnp.bfloat16)

    def sum_all(spread):
        total = wide(spread[0])
        for i in range(1, spread.shape[0]):
            total = total + wide(spread[i])
        return total

    def take(parts, step):
        z = (my_z + step) % 4
        some = lax.dynamic_slice_in_dim(parts, z % 2, 1, axis=-5)
        some = lax.dynamic_slice_in_dim(some, z // 2, 1, axis=-3)
        return some.reshape(-1, ROWS, parts.shape[-1])

    def sum_z(own_part, others):
        total = wide(own_part)
        for step, part in others:
            total = total + wide(move(part, z=step))
        return total.astype(jnp.bfloat16)

    first = partial[:, : rank // 2].reshape(4, -1, rank // 2)
    first = sum_all(exchange(first, along_y)).astype(jnp.bfloat16)
    second = partial.reshape(4, LO, X, 2, ROWS, rank)
    others = [(step, take(second, step)[:, :, rank // 2 :]) for step in (1, 3, 2)]
    second = sum_z(take(second, 0)[:, :, rank // 2 :], others)
    w_up, w_down, w_z = together(w_up, w_down, w_z, after=[part for _, part in others])
    zx_up = move(w_z, x=-1)
    zx_down = move(w_z, x=1)
    steps = [(0, 0), (0, 1), (0, 3), (1, 0), (1, 1), (1, 3), (0, 2), (1, 2)]
    at = shard.reshape(1)
    other_near, own_near = keys_of([other, own], at, steps[:4], [half, w_up, w_down, w_z])
    second, w_far = together(second, jnp.where(core == 0, w_up, w_down), after=(own_near,))
    w_far = move_apart(w_far, x=-1)
    second = sum_all(exchange(second.reshape(4, X * ROWS, rank // 2), along_y)).astype(jnp.bfloat16)
    first = first.reshape(LO, X, 2, ROWS, rank // 2)
    others = [(step, take(first, step)) for step in (1, 3, 2)]
    first = sum_z(take(first, 0), others)
    w_far, zx_up, zx_down = together(w_far, zx_up, zx_down, after=[part for _, part in others])
    zx_far = move_apart(w_far, z=-1)
    both = jnp.concatenate([first.reshape(X, ROWS, -1), second.reshape(X, ROWS, -1)], axis=2)
    projected = sum_all(exchange(both, along_x))
    new_avg = 0.9 * exp_avg + 0.1 * projected
    new_sq = 0.999 * exp_avg_sq + 0.001 * projected * projected
    first_fix = 1.0 - 0.9**STEP
    second_fix = 1.0 - 0.999**STEP
    direction = new_avg / first_fix / (jnp.sqrt(new_sq / second_fix) + 1e-08)
    direction = direction.astype(jnp.bfloat16)
    for_other, own_keys = keys_of(
        [other, own], at, steps[4:], [zx_up, zx_down, w_far, zx_far], [other_near, own_near], (direction,)
    )

    mine = exchange(jnp.broadcast_to(direction[None], (chips, ROWS, rank)), same_shard)
    theirs = move(mine, core=1)
    (for_other,) = together(for_other, after=(mine,))
    keys = (own_keys + move(for_other, core=1)).astype(jnp.bfloat16)
    even = jnp.where(core == 0, mine, theirs)
    odd = jnp.where(core == 0, theirs, mine)
    update = lax.dot_general(
        jnp.stack([even, odd], axis=1).reshape(-1, rank),
        basis,
        (((1,), (1,)), ((), ())),
        preferred_element_type=jnp.float32,
    )
    new_weight = (wide(weight) - learn_rate * galore_scale * update).astype(jnp.bfloat16)
    return (keys, new_weight, new_avg, new_sq)


def solution(mesh):
    in_specs = (
        P(("dp", "fsdp"), None),
        P(("dp", "fsdp"), None),
        P("fsdp", None),
        P(),
        P(("fsdp", "dp"), None),
        P(("fsdp", "dp"), None),
    )
    out_specs = (
        P(("dp", "fsdp"), None),
        P("fsdp", None),
        P(("fsdp", "dp"), None),
        P(("fsdp", "dp"), None),
    )
    return jax.shard_map(local, mesh=mesh, in_specs=in_specs, out_specs=out_specs, check_vma=False)
```
